512 devices in a mesh: row: 16 (over y, z_hi), col: 32 (over x, z_lo, core).
Axes of the slice: x: 4, y: 8, z: 8 (z_hi: 2, z_lo: 4; z = z_hi * 4 + z_lo), core: 2. Of those that a mesh axis runs over, the one named last changes fastest.
Arguments:
- factor: bfloat16 [28672, 28672], P('row', 'col'), may hold values from -2 to 2, as said below
- gradient: float32 [28672, 2048], P(('row', 'col')), may hold values from -6 to 6
- starts: int32 [16], replicated, may hold values from 0 to 15, each once
Outputs:
- solved: float32 [28672, 2048], P(('row', 'col'))
The draws below stay inside these ranges and needn't reach their ends.
Inputs may be any that keep to these rules, and one draw needn't show every extreme that they name: `factor`: tiles above the block diagonal are zero, and every diagonal tile is upper triangular. `starts`: every block column is the start of exactly one panel.
All inputs are finite; a program needn't handle non-finite values.
Results may differ from the reference program's by a relative error of at most 0.0046.
Values may be sent and summed in bfloat16 or wider, within the bound.
A program may use at most 64 MiB of HBM per device.

```python
import math
import jax
import jax.numpy as jnp
from jax import lax

TILE = 1792
PANEL = 128
TICKS = 6
BLOCKS = 16
ORDER = 28672


def draw_factor(key, part):
    noise_key, diag_key = jax.random.split(jax.random.fold_in(key, 17))
    noise_draw = jax.random.normal(noise_key, (ORDER, ORDER), jnp.float32)
    scales = jnp.exp(jax.random.uniform(diag_key, (ORDER,), jnp.float32, math.log(0.5), math.log(2.0)))
    row_ids = lax.broadcasted_iota(jnp.int32, (ORDER, ORDER), 0)
    col_ids = lax.broadcasted_iota(jnp.int32, (ORDER, ORDER), 1)
    below_blocks = row_ids // TILE > col_ids // TILE
    inside = (row_ids // TILE == col_ids // TILE) & (row_ids < col_ids)
    scaled = noise_draw * (0.5 / math.sqrt(TILE))
    values = jnp.where(below_blocks | inside, scaled, 0.0)
    values = values + jnp.where(row_ids == col_ids, scales[None, :], 0.0)
    return values.astype(jnp.bfloat16)


def steps_of(stream_key, extent, cuts, least, top_value):
    loudness = 1.0
    for position, parts in cuts:
        draws = jax.random.uniform(jax.random.fold_in(jax.random.fold_in(stream_key, 6), position), (parts,), jnp.float32, least / len(cuts), top_value / len(cuts))
        loudness = loudness * jnp.repeat(jnp.exp(draws), extent[position] // parts).reshape((-1,) + (1,) * (len(extent) - 1 - position))
    return loudness


def normal_values(rng, extent, width, most, cuts=(), held_as=jnp.bfloat16):
    values = jax.random.normal(rng, extent, jnp.float32) * width
    if len(cuts) > 0:
        values = steps_of(rng, extent, cuts, -0.22, 0.18) * values
    return jnp.clip(values, min=-most, max=most).astype(held_as)


def setup_inputs(seed: int = 0) -> dict:
    keys = jax.random.split(jax.random.key(seed), 4)
    factor = draw_factor(jax.random.fold_in(keys[3], 71), 0)
    gradient = normal_values(keys[1], (ORDER, BLOCKS * PANEL), 1.0, 6.0, ((0, 512),), jnp.float32)
    starts = jax.random.permutation(keys[2], BLOCKS).astype(jnp.int32)
    return dict(factor=factor, gradient=gradient, starts=starts)


def reference(factor, gradient, starts):
    panels = gradient.reshape(ORDER, BLOCKS, PANEL).transpose(1, 0, 2)
    row_ids = jnp.arange(ORDER, dtype=jnp.int32)[:, None]

    def solve_panel(inputs):
        residual, start = inputs
        for tick_idx in range(TICKS):
            block_idx = start + tick_idx
            valid = block_idx < BLOCKS
            clamped = jnp.minimum(block_idx, BLOCKS - 1).astype(jnp.int32)
            begin = (clamped * TILE).astype(jnp.int32)
            column = lax.dynamic_slice_in_dim(factor, begin, TILE, 1)
            diag_tile = lax.dynamic_slice_in_dim(column, begin, TILE, 0)
            current = lax.dynamic_slice_in_dim(residual, begin, TILE, 0).astype(jnp.bfloat16)
            solution = jnp.dot(diag_tile.T, current, preferred_element_type=jnp.float32)
            update = jnp.dot(column, solution.astype(jnp.bfloat16), preferred_element_type=jnp.float32)
            below_rows = row_ids >= begin + TILE
            residual = jnp.where(valid & below_rows, residual - update, residual)
            written = lax.dynamic_update_slice_in_dim(residual, solution, begin, 0)
            residual = jnp.where(valid, written, residual)
        return residual

    result = lax.map(solve_panel, (panels, starts))
    return result.transpose(1, 0, 2).reshape(ORDER, BLOCKS * PANEL)
```

```python
import functools
import jax
import jax.numpy as jnp
from jax import lax
from jax.experimental import pallas as pl
from jax.experimental.pallas import tpu as pltpu
from jax.sharding import PartitionSpec as P

TICKS = 6
CHUNKS = 2
MESH = pl.DeviceIdType.MESH
F32 = jnp.float32
BF16 = jnp.bfloat16


def kernel(
    blocks, starts_ref, grad_ref, factor_ref, out_ref,
    tile, raw, diag, vec, res, solved, partial, sums, tail, grad_given, grad_own, grad_send, grad_in, x_ret, x_in, tail_in,
    load_sem, tile_sem, us_sem, u_sem, gs_sem, g_sem, vs_sem, v_sem, xs_sem, qs_sem, q_sem,
    ss_sem, s_sem, rs_sem, r_sem, ts_sem, t_sem,
):
    row = lax.axis_index("row")
    col = lax.axis_index("col")
    blk = col // 2
    half = col % 2
    owners = blocks
    rows = grad_ref.shape[0]
    width = grad_ref.shape[1] // blocks
    half_rows = factor_ref.shape[1]
    step = half_rows // CHUNKS
    group = owners // CHUNKS
    lanes = 128
    per = half_rows // lanes
    sib = col + 1 - 2 * half
    other = 1 - half
    is_diag = row == blk
    is_next = row == blk + 1
    is_lower = row > blk
    my_group = col // owners
    diag_core = 2 * row + my_group
    next_core = jnp.where(row > 0, diag_core - 2, diag_core)

    own_rows = pl.ds(pl.multiple_of(half * half_rows, half_rows), half_rows)
    other_rows = pl.ds(pl.multiple_of(other * half_rows, half_rows), half_rows)
    load_raw = pltpu.make_async_copy(factor_ref, raw, load_sem)
    load_half = pltpu.make_async_copy(factor_ref.at[own_rows], tile.at[half], load_sem)

    @pl.when(is_diag)
    def _():
        load_raw.start()

    @pl.when(is_lower)
    def _():
        load_half.start()

    barrier = pltpu.get_barrier_semaphore()

    @pl.loop(0, 2 * blocks)
    def _(c):
        @pl.when(c != col)
        def _():
            pl.semaphore_signal(barrier, inc=1, device_id=(row, c), device_id_type=MESH)

    far = [(1, 0), (2, 0), (-1, 0), (-2, 0), (1, 2), (2, 2), (-1, -2), (-2, -2)]
    for dr, dc in far:
        pl.semaphore_signal(
            barrier, inc=1, device_id=((row + dr + blocks) % blocks, (col + dc + 2 * blocks) % (2 * blocks)),
            device_id_type=MESH,
        )

    for p in range(blocks):
        grad_given[p] = grad_ref[:, p * width:(p + 1) * width]
    for s in range(blocks):
        which = jnp.int32(0)
        for p in range(blocks):
            which = which + jnp.where(starts_ref[p] == s, p, 0)
        grad_own[s] = grad_given[jnp.minimum(which, blocks - 1)]
    pad = jnp.zeros((64 - rows, width), F32)

    @pl.loop(0, TICKS)
    def _(t):
        @pl.when(row >= t)
        def _():
            grad_send[t] = jnp.concatenate([grad_own[row - t], pad], axis=0).astype(BF16)

        @pl.when(row < t)
        def _():
            grad_send[t] = jnp.zeros((64, width), BF16)

    pl.semaphore_wait(barrier, 2 * blocks - 1 + len(far))

    my_slot = col % owners
    pieces = ((0, 1, diag_core), (1, TICKS - 1, next_core))

    def grad_copy(k):
        lo, n, target = pieces[k]
        return pltpu.make_async_remote_copy(
            src_ref=grad_send.at[pl.ds(lo, n)],
            dst_ref=grad_in.at[pl.ds(lo, n), my_slot],
            send_sem=gs_sem.at[k], recv_sem=g_sem.at[k],
            device_id=(row, target), device_id_type=MESH,
        )

    def grad_local(k):
        lo, n, target = pieces[k]
        return pltpu.make_async_copy(
            grad_send.at[pl.ds(lo, n)], grad_in.at[pl.ds(lo, n), my_slot], g_sem.at[k]
        )

    def wait_grad(k):
        lo, n, target = pieces[k]
        pltpu.make_async_copy(grad_in.at[pl.ds(lo, n)], grad_in.at[pl.ds(lo, n)], g_sem.at[k]).wait()

    grad_goes = (row >= 0, row > 0)
    for k in range(2):
        @pl.when(grad_goes[k] & (col != pieces[k][2]))
        def _():
            grad_copy(k).start()

        @pl.when(grad_goes[k] & (col == pieces[k][2]))
        def _():
            grad_local(k).start()

    def diag_copy(h, k):
        part = (pl.ds(0, h * half_rows + (k + 1) * lanes), pl.ds(k * lanes, lanes))
        return pltpu.make_async_remote_copy(
            src_ref=factor_ref.at[part], dst_ref=raw.at[part],
            send_sem=us_sem.at[k], recv_sem=u_sem.at[k],
            device_id=(row, (col - 2 + 2 * blocks) % (2 * blocks)), device_id_type=MESH,
        )

    for h in range(2):
        @pl.when(is_diag & (row > 0) & (half == h))
        def _():
            for k in range(per):
                diag_copy(h, k).start()

    tile_copy = pltpu.make_async_remote_copy(
        src_ref=factor_ref.at[other_rows], dst_ref=tile.at[half],
        send_sem=tile_sem.at[0], recv_sem=tile_sem.at[1],
        device_id=(row, sib), device_id_type=MESH,
    )

    @pl.when(is_lower)
    def _():
        tile_copy.start()

    def lay_diag(k):
        m = slice(k * lanes, (k + 1) * lanes)

        @pl.loop(0, 2 * per)
        def _(n):
            src = pl.ds(pl.multiple_of(n * lanes, lanes), lanes)
            dst = pl.ds(pl.multiple_of((n % per) * lanes, lanes), lanes)

            @pl.when(n <= half * per + k)
            def _():
                diag[n // per, m, dst] = raw[src, m].T

            @pl.when(n > half * per + k)
            def _():
                diag[n // per, m, dst] = jnp.zeros((lanes, lanes), BF16)

    def chunk(m):
        return pl.ds(pl.multiple_of(m * step, step), step)

    def sibling_copy(ref, t, m, send_sem, recv_sem):
        part = ref.at[t, half, chunk(m)]
        return pltpu.make_async_remote_copy(
            src_ref=part, dst_ref=part, send_sem=send_sem.at[t, m], recv_sem=recv_sem.at[t, m],
            device_id=(row, sib), device_id_type=MESH,
        )

    def vec_copy(t, m):
        return sibling_copy(vec, t, m, vs_sem.at[0], v_sem.at[0])

    def res_copy(t, m):
        return sibling_copy(res, t, m, qs_sem, q_sem)

    def forward_copy(t, m):
        part = vec.at[t, half, chunk(m)]
        return pltpu.make_async_remote_copy(
            src_ref=part, dst_ref=part, send_sem=vs_sem.at[1, t, m], recv_sem=v_sem.at[1, t, m],
            device_id=((row + 2) % blocks, col), device_id_type=MESH,
        )

    def solved_copy(t, m, k):
        return pltpu.make_async_remote_copy(
            src_ref=solved.at[t, chunk(m)], dst_ref=vec.at[t, half, chunk(m)],
            send_sem=xs_sem.at[k - 1, t, m], recv_sem=v_sem.at[1, t, m],
            device_id=((row + k) % blocks, 2 * row + half), device_id_type=MESH,
        )

    def partial_copy(t, m):
        return pltpu.make_async_remote_copy(
            src_ref=sums.at[t, chunk(m)], dst_ref=partial.at[(t + 1) % TICKS, chunk(m)],
            send_sem=ss_sem.at[t, m], recv_sem=s_sem.at[(t + 1) % TICKS, m],
            device_id=(row, (col + 2) % (2 * blocks)), device_id_type=MESH,
        )

    def wait_partial(t, m):
        pltpu.make_async_copy(partial.at[t, chunk(m)], partial.at[t, chunk(m)], s_sem.at[t, m]).wait()

    padding = jnp.zeros((group, 64 - rows, width), F32)

    def laid(y):
        return jnp.concatenate([y.reshape(group, rows, width), padding], axis=1).astype(BF16)

    def given(t, m):
        return grad_in[t, m * group:(m + 1) * group].astype(F32)[:, :rows].reshape(step, width)

    def solve(t):
        for m in range(CHUNKS):
            res_copy(t, m).wait_recv()
        for m in range(CHUNKS):
            x = jnp.dot(diag[0, chunk(m)], res[t, 0], preferred_element_type=F32)
            x = x + jnp.dot(diag[1, chunk(m)], res[t, 1], preferred_element_type=F32)
            solved[t, chunk(m)] = x.astype(BF16)
            for k in (1, 2):
                @pl.when(row + k < blocks)
                def _():
                    solved_copy(t, m, k).start()
            x_ret[t, m * group:(m + 1) * group] = laid(x)

    @pl.when(is_diag)
    def _():
        load_raw.wait()
        for k in range(per):
            lay_diag(k)
        wait_grad(0)
        for m in range(CHUNKS):
            res[0, half, chunk(m)] = given(0, m).astype(BF16)
            res_copy(0, m).start()
        solve(0)

    @pl.when(is_lower)
    def _():
        load_half.wait()
        tile_copy.wait_recv()

    def give(o, src, dst, send_sem, recv_sem):
        target = half * owners + o

        @pl.when(target != col)
        def _():
            pltpu.make_async_remote_copy(
                src_ref=src, dst_ref=dst, send_sem=send_sem, recv_sem=recv_sem,
                device_id=(row, target), device_id_type=MESH,
            ).start()

        @pl.when(target == col)
        def _():
            pltpu.make_async_copy(src, dst, recv_sem).start()

    slot = jnp.clip(blk - (TICKS - 1), 0, tail_in.shape[0] - 1)
    rest = pl.ds(1, TICKS - 1)

    @pl.when(is_diag)
    def _():
        @pl.loop(0, owners)
        def _(o):
            give(o, x_ret.at[0, o], x_in.at[0], rs_sem, r_sem.at[0])

    def tick(t):
        for m in range(CHUNKS):
            solved_copy(t, m, 1).wait_recv()

            @pl.when(row + 2 < blocks)
            def _():
                forward_copy(t, m).start()

            vec_copy(t, m).start()

        for m in range(CHUNKS):
            vec_copy(t, m).wait_recv()

        @pl.when(is_next & (t == 0))
        def _():
            wait_grad(1)

        for m in range(CHUNKS):
            y = jnp.dot(tile[0, chunk(m)], vec[t, 0], preferred_element_type=F32)
            y = y + jnp.dot(tile[1, chunk(m)], vec[t, 1], preferred_element_type=F32)
            sums[t, chunk(m)] = y

            @pl.when(t > 0)
            def _():
                wait_partial(t, m)
                sums[t, chunk(m)] = sums[t, chunk(m)] + partial[t, chunk(m)]

            @pl.when(t == TICKS - 1)
            def _():
                tail[m * group:(m + 1) * group] = laid(sums[t, chunk(m)])

            @pl.when((t < TICKS - 1) & jnp.logical_not(is_next))
            def _():
                partial_copy(t, m).start()

            @pl.when((t < TICKS - 1) & is_next)
            def _():
                after = jnp.minimum(t + 1, TICKS - 1)
                res[after, half, chunk(m)] = (given(after, m) - sums[t, chunk(m)]).astype(BF16)
                res_copy(after, m).start()

        @pl.when(is_next & (t < TICKS - 1))
        def _():
            @pl.when(t == 0)
            def _():
                for k in range(per):
                    for h in range(2):
                        @pl.when(half == h)
                        def _():
                            diag_copy(h, k).wait_recv()
                    lay_diag(k)

            solve(jnp.minimum(t + 1, TICKS - 1))

    @pl.loop(0, TICKS)
    def _(t):
        @pl.when(is_next & (t == TICKS - 1))
        def _():
            @pl.loop(0, owners)
            def _(o):
                give(o, x_ret.at[rest, o], x_in.at[rest], rs_sem, r_sem.at[1])

        @pl.when(is_lower & (blk >= t))
        def _():
            tick(t)

    has_tail = is_lower & (blk >= TICKS - 1)

    @pl.when(has_tail)
    def _():
        @pl.loop(0, owners)
        def _(o):
            give(o, tail.at[o], tail_in.at[slot], ts_sem, t_sem.at[slot])

    pltpu.make_async_copy(x_in.at[0], x_in.at[0], r_sem.at[0]).wait()

    @pl.when(row > 0)
    def _():
        pltpu.make_async_copy(x_in.at[rest], x_in.at[rest], r_sem.at[1]).wait()

    @pl.loop(0, blocks)
    def _(s):
        t = row - s

        @pl.when((t >= 0) & (t < TICKS))
        def _():
            grad_own[s] = x_in[jnp.clip(t, 0, TICKS - 1)].astype(F32)[:rows]

        @pl.when(t >= TICKS)
        def _():
            ref = tail_in.at[jnp.minimum(s, tail_in.shape[0] - 1)]
            pltpu.make_async_copy(ref, ref, t_sem.at[jnp.minimum(s, tail_in.shape[0] - 1)]).wait()
            grad_own[s] = grad_own[s] - ref[...].astype(F32)[:rows]

    for p in range(blocks):
        out_ref[:, p * width:(p + 1) * width] = grad_own[starts_ref[p]]

    for k in range(2):
        @pl.when(grad_goes[k] & (col != pieces[k][2]))
        def _():
            grad_copy(k).wait_send()

    for h in range(2):
        @pl.when(is_diag & (row > 0) & (half == h))
        def _():
            for k in range(per):
                diag_copy(h, k).wait_send()

    @pl.when(is_lower)
    def _():
        tile_copy.wait_send()

    @pl.loop(0, TICKS)
    def _(t):
        for m in range(CHUNKS):
            @pl.when((is_diag & (t == 0)) | (is_next & (t > 0) & (row >= t)))
            def _():
                res_copy(t, m).wait_send()
                for k in (1, 2):
                    @pl.when(row + k < blocks)
                    def _():
                        solved_copy(t, m, k).wait_send()

            @pl.when(is_lower & (blk >= t))
            def _():
                vec_copy(t, m).wait_send()

                @pl.when(row + 2 < blocks)
                def _():
                    forward_copy(t, m).wait_send()

                @pl.when((t < TICKS - 1) & jnp.logical_not(is_next))
                def _():
                    partial_copy(t, m).wait_send()

    def sent_all(ref_all, ref_less, sem):
        @pl.when(my_group == half)
        def _():
            pltpu.make_async_copy(ref_less, ref_less, sem).wait()

        @pl.when(my_group != half)
        def _():
            pltpu.make_async_copy(ref_all, ref_all, sem).wait()

    less = pl.ds(0, owners - 1)

    @pl.when(has_tail)
    def _():
        sent_all(tail, tail.at[less], ts_sem)

    @pl.when(is_diag)
    def _():
        sent_all(x_ret.at[0], x_ret.at[0, less], rs_sem)

    @pl.when(is_next)
    def _():
        sent_all(x_ret.at[rest], x_ret.at[rest, less], rs_sem)


def body(factor, gradient, starts):
    blocks = starts.shape[0]
    rows = gradient.shape[0]
    width = gradient.shape[1] // blocks
    tile_rows, half_rows = factor.shape
    owners = blocks
    vmem = pltpu.VMEM
    dma = pltpu.SemaphoreType.DMA
    spare = max(blocks - TICKS, 1)
    scratch = [
        vmem((2, half_rows, half_rows), BF16),
        vmem((tile_rows, half_rows), BF16),
        vmem((2, half_rows, half_rows), BF16),
        vmem((TICKS, 2, half_rows, width), BF16),
        vmem((TICKS, 2, half_rows, width), BF16),
        vmem((TICKS, half_rows, width), BF16),
        vmem((TICKS, half_rows, width), F32),
        vmem((TICKS, half_rows, width), F32),
        vmem((owners, 64, width), BF16),
        vmem((blocks, rows, width), F32),
        vmem((blocks, rows, width), F32),
        vmem((TICKS, 64, width), BF16),
        vmem((TICKS, owners, 64, width), BF16),
        vmem((TICKS, owners, 64, width), BF16),
        vmem((TICKS, 64, width), BF16),
        vmem((spare, 64, width), BF16),
        dma, dma((2,)), dma((half_rows // 128,)), dma((half_rows // 128,)), dma((2,)), dma((2,)),
        dma((2, TICKS, CHUNKS)), dma((2, TICKS, CHUNKS)), dma((2, TICKS, CHUNKS)),
        dma((TICKS, CHUNKS)), dma((TICKS, CHUNKS)), dma((TICKS, CHUNKS)), dma((TICKS, CHUNKS)),
        dma, dma((2,)), dma, dma((spare,)),
    ]
    return pl.pallas_call(
        functools.partial(kernel, blocks),
        out_shape=jax.ShapeDtypeStruct(gradient.shape, F32),
        in_specs=[
            pl.BlockSpec(memory_space=pltpu.SMEM),
            pl.BlockSpec(memory_space=pltpu.VMEM),
            pl.BlockSpec(memory_space=pl.ANY),
        ],
        out_specs=pl.BlockSpec(memory_space=pltpu.VMEM),
        scratch_shapes=scratch,
        compiler_params=pltpu.CompilerParams(
            collective_id=0, has_side_effects=True, vmem_limit_bytes=62 * 1024 * 1024
        ),
        cost_estimate=pl.CostEstimate(
            flops=2 * TICKS * tile_rows * half_rows * width,
            bytes_accessed=2 * tile_rows * half_rows, transcendentals=0,
        ),
    )(starts, gradient, factor)


def solution(mesh):
    in_specs = (P("row", "col"), P(("row", "col"), None), P())
    out_specs = P(("row", "col"), None)
    return jax.shard_map(body, mesh=mesh, in_specs=in_specs, out_specs=out_specs, check_vma=False)
```

```python
import functools
import jax
import jax.numpy as jnp
from jax import lax
from jax.experimental import pallas as pl
from jax.experimental.pallas import tpu as pltpu
from jax.sharding import PartitionSpec as P

TICKS = 6
CHUNKS = 2
MESH = pl.DeviceIdType.MESH
F32 = jnp.float32
BF16 = jnp.bfloat16


def kernel(
    blocks, starts_ref, grad_ref, factor_ref, out_ref,
    tile, raw, diag, vec, res, solved, partial, sums, near, near_sums, first, first_in,
    tail, grad_given, grad_own, grad_send, grad_in, x_ret, x_in, tail_in,
    load_sem, tile_sem, us_sem, u_sem, gs_sem, g_sem, vs_sem, v_sem, xs_sem, qs_sem, q_sem,
    ss_sem, s_sem, fs_sem, f_sem, rs_sem, r_sem, ts_sem, t_sem,
):
    row = lax.axis_index("row")
    col = lax.axis_index("col")
    blk = col // 2
    half = col % 2
    owners = blocks
    rows = grad_ref.shape[0]
    width = grad_ref.shape[1] // blocks
    half_rows = factor_ref.shape[1]
    step = half_rows // CHUNKS
    group = owners // CHUNKS
    lanes = 128
    per = half_rows // lanes
    sib = col + 1 - 2 * half
    other = 1 - half
    is_diag = row == blk
    is_next = row == blk + 1
    is_lower = row > blk
    is_upper = row < blk
    apart = row % 4 == 0
    moved = jnp.logical_not(apart)
    my_group = col // owners
    diag_core = 2 * row + my_group
    next_core = jnp.where(row > 0, diag_core - 2, diag_core)

    own_rows = pl.ds(pl.multiple_of(half * half_rows, half_rows), half_rows)
    other_rows = pl.ds(pl.multiple_of(other * half_rows, half_rows), half_rows)
    load_raw = pltpu.make_async_copy(factor_ref, raw, load_sem)
    load_half = pltpu.make_async_copy(factor_ref.at[own_rows], tile.at[half], load_sem)

    @pl.when(is_diag)
    def _():
        load_raw.start()

    @pl.when(is_lower)
    def _():
        load_half.start()

    barrier = pltpu.get_barrier_semaphore()

    @pl.loop(0, 2 * blocks)
    def _(c):
        @pl.when(c != col)
        def _():
            pl.semaphore_signal(barrier, inc=1, device_id=(row, c), device_id_type=MESH)

    far = [(1, 0), (2, 0), (-1, 0), (-2, 0), (1, 2), (2, 2), (-1, -2), (-2, -2)]
    for dr, dc in far:
        pl.semaphore_signal(
            barrier, inc=1, device_id=((row + dr + blocks) % blocks, (col + dc + 2 * blocks) % (2 * blocks)),
            device_id_type=MESH,
        )

    for p in range(blocks):
        grad_given[p] = grad_ref[:, p * width:(p + 1) * width]
    for s in range(blocks):
        which = jnp.int32(0)
        for p in range(blocks):
            which = which + jnp.where(starts_ref[p] == s, p, 0)
        grad_own[s] = grad_given[jnp.minimum(which, blocks - 1)]
    pad = jnp.zeros((64 - rows, width), F32)

    @pl.loop(0, TICKS)
    def _(t):
        @pl.when(row >= t)
        def _():
            grad_send[t] = jnp.concatenate([grad_own[row - t], pad], axis=0).astype(BF16)

        @pl.when(row < t)
        def _():
            grad_send[t] = jnp.zeros((64, width), BF16)

    pl.semaphore_wait(barrier, 2 * blocks - 1 + len(far))

    my_slot = col % owners
    pieces = ((0, 1, diag_core), (1, 1, diag_core), (2, TICKS - 2, jnp.where(apart, diag_core, next_core)))

    def grad_copy(k):
        lo, n, target = pieces[k]
        return pltpu.make_async_remote_copy(
            src_ref=grad_send.at[pl.ds(lo, n)],
            dst_ref=grad_in.at[pl.ds(lo, n), my_slot],
            send_sem=gs_sem.at[k], recv_sem=g_sem.at[k],
            device_id=(row, target), device_id_type=MESH,
        )

    def grad_local(k):
        lo, n, target = pieces[k]
        return pltpu.make_async_copy(
            grad_send.at[pl.ds(lo, n)], grad_in.at[pl.ds(lo, n), my_slot], g_sem.at[k]
        )

    def wait_grad(k):
        lo, n, target = pieces[k]
        pltpu.make_async_copy(grad_in.at[pl.ds(lo, n)], grad_in.at[pl.ds(lo, n)], g_sem.at[k]).wait()

    def send_grad(k):
        @pl.when(col != pieces[k][2])
        def _():
            grad_copy(k).start()

        @pl.when(col == pieces[k][2])
        def _():
            grad_local(k).start()

    send_grad(0)
    send_grad(1)

    @pl.when(row > 0)
    def _():
        send_grad(2)

    def diag_copy(h, k):
        part = (pl.ds(0, h * half_rows + (k + 1) * lanes), pl.ds(k * lanes, lanes))
        return pltpu.make_async_remote_copy(
            src_ref=factor_ref.at[part], dst_ref=raw.at[part],
            send_sem=us_sem.at[k], recv_sem=u_sem.at[k],
            device_id=(row, (col - 2 + 2 * blocks) % (2 * blocks)), device_id_type=MESH,
        )

    for h in range(2):
        @pl.when(is_diag & moved & (half == h))
        def _():
            for k in range(per):
                diag_copy(h, k).start()

    tile_copy = pltpu.make_async_remote_copy(
        src_ref=factor_ref.at[other_rows], dst_ref=tile.at[half],
        send_sem=tile_sem.at[0], recv_sem=tile_sem.at[1],
        device_id=(row, sib), device_id_type=MESH,
    )

    @pl.when(is_lower)
    def _():
        tile_copy.start()

    def lay_diag(k):
        m = slice(k * lanes, (k + 1) * lanes)

        @pl.loop(0, 2 * per)
        def _(n):
            src = pl.ds(pl.multiple_of(n * lanes, lanes), lanes)
            dst = pl.ds(pl.multiple_of((n % per) * lanes, lanes), lanes)

            @pl.when(n <= half * per + k)
            def _():
                diag[n // per, m, dst] = raw[src, m].T

            @pl.when(n > half * per + k)
            def _():
                diag[n // per, m, dst] = jnp.zeros((lanes, lanes), BF16)

    def chunk(m):
        return pl.ds(pl.multiple_of(m * step, step), step)

    def sibling_copy(ref, t, m, send_sem, recv_sem):
        part = ref.at[t, half, chunk(m)]
        return pltpu.make_async_remote_copy(
            src_ref=part, dst_ref=part, send_sem=send_sem.at[t, m], recv_sem=recv_sem.at[t, m],
            device_id=(row, sib), device_id_type=MESH,
        )

    def vec_copy(t, m):
        return sibling_copy(vec, t, m, vs_sem.at[0], v_sem.at[0])

    def res_copy(t, m):
        return sibling_copy(res, t, m, qs_sem, q_sem)

    def forward_copy(t, m):
        part = vec.at[t, half, chunk(m)]
        return pltpu.make_async_remote_copy(
            src_ref=part, dst_ref=part, send_sem=vs_sem.at[1, t, m], recv_sem=v_sem.at[1, t, m],
            device_id=((row + 2) % blocks, col), device_id_type=MESH,
        )

    def solved_copy(t, m, k):
        return pltpu.make_async_remote_copy(
            src_ref=solved.at[t, chunk(m)], dst_ref=vec.at[t, half, chunk(m)],
            send_sem=xs_sem.at[k, t, m], recv_sem=v_sem.at[1, t, m],
            device_id=((row + 1 + k) % blocks, 2 * row + half), device_id_type=MESH,
        )

    into_next = row == blk + 2
    right = (row, (col + 2) % (2 * blocks))

    def partial_copy(t, m, src, dst, k):
        return pltpu.make_async_remote_copy(
            src_ref=src.at[t, chunk(m)], dst_ref=dst.at[(t + 1) % TICKS, chunk(m)],
            send_sem=ss_sem.at[k, t, m], recv_sem=s_sem.at[k, (t + 1) % TICKS, m],
            device_id=right, device_id_type=MESH,
        )

    def far_sum(t, m):
        return partial_copy(t, m, sums, partial, 0)

    def near_sum(t, m):
        return partial_copy(t, m, near_sums, near, 1)

    def wait_sum(ref, t, m, k):
        pltpu.make_async_copy(ref.at[t, chunk(m)], ref.at[t, chunk(m)], s_sem.at[k, t, m]).wait()

    def first_copy(t, m):
        return pltpu.make_async_remote_copy(
            src_ref=first.at[t, chunk(m)], dst_ref=first_in.at[t, chunk(m)],
            send_sem=fs_sem.at[t, m], recv_sem=f_sem.at[t, m], device_id=right, device_id_type=MESH,
        )

    padding = jnp.zeros((group, 64 - rows, width), F32)

    def laid(y):
        return jnp.concatenate([y.reshape(group, rows, width), padding], axis=1).astype(BF16)

    def given(t, m):
        return grad_in[t, m * group:(m + 1) * group].astype(F32)[:, :rows].reshape(step, width)

    def solve(t):
        for m in range(CHUNKS):
            res_copy(t, m).wait_recv()
        for m in range(CHUNKS):
            x = jnp.dot(diag[0, chunk(m)], res[t, 0], preferred_element_type=F32)
            x = x + jnp.dot(diag[1, chunk(m)], res[t, 1], preferred_element_type=F32)
            solved[t, chunk(m)] = x.astype(BF16)
            for k in range(2):
                @pl.when(row + 1 + k < blocks)
                def _():
                    solved_copy(t, m, k).start()
            x_ret[t, m * group:(m + 1) * group] = laid(x)

    def give(o, src, dst, send_sem, recv_sem):
        target = half * owners + o

        @pl.when(target != col)
        def _():
            pltpu.make_async_remote_copy(
                src_ref=src, dst_ref=dst, send_sem=send_sem, recv_sem=recv_sem,
                device_id=(row, target), device_id_type=MESH,
            ).start()

        @pl.when(target == col)
        def _():
            pltpu.make_async_copy(src, dst, recv_sem).start()

    slot = jnp.clip(blk - (TICKS - 1), 0, tail_in.shape[0] - 1)
    start = pl.ds(0, 2)
    rest = pl.ds(2, TICKS - 2)

    def give_rest():
        @pl.loop(0, owners)
        def _(o):
            give(o, x_ret.at[rest, o], x_in.at[rest], rs_sem.at[1], r_sem.at[1])

    def solve_apart(t):
        for m in range(CHUNKS):
            first_copy(t, m).wait_recv()
            res[t, half, chunk(m)] = (given(t, m) - first_in[t, chunk(m)].astype(F32)).astype(BF16)
            res_copy(t, m).start()
        solve(t)

    @pl.when(is_diag)
    def _():
        load_raw.wait()
        for k in range(per):
            lay_diag(k)
        wait_grad(0)
        for m in range(CHUNKS):
            res[0, half, chunk(m)] = given(0, m).astype(BF16)
            res_copy(0, m).start()
        solve(0)
        wait_grad(1)

        @pl.when(row > 0)
        def _():
            solve_apart(1)

        @pl.loop(0, owners)
        def _(o):
            give(o, x_ret.at[start, o], x_in.at[start], rs_sem.at[0], r_sem.at[0])

        @pl.when(apart & (row > 0))
        def _():
            wait_grad(2)

            @pl.loop(2, TICKS)
            def _(t):
                @pl.when(row >= t)
                def _():
                    solve_apart(t)

            give_rest()

    @pl.when(is_lower)
    def _():
        partial[0] = jnp.zeros_like(partial[0])
        near[0] = jnp.zeros_like(near[0])
        load_half.wait()
        tile_copy.wait_recv()

    def wait_start():
        pltpu.make_async_copy(x_in.at[start], x_in.at[start], r_sem.at[0]).wait()

    @pl.when(is_upper)
    def _():
        wait_start()

    def lay_blocks(lo, hi):
        for k in range(lo, hi):
            for h in range(2):
                @pl.when(half == h)
                def _():
                    diag_copy(h, k).wait_recv()
            lay_diag(k)

    def product(t, m):
        y = jnp.dot(tile[0, chunk(m)], vec[t, 0], preferred_element_type=F32)
        return y + jnp.dot(tile[1, chunk(m)], vec[t, 1], preferred_element_type=F32)

    def tick(t):
        for m in range(CHUNKS):
            forward_copy(t, m).wait_recv()

            @pl.when(row + 2 < blocks)
            def _():
                forward_copy(t, m).start()

            vec_copy(t, m).start()

        for m in range(CHUNKS):
            vec_copy(t, m).wait_recv()

        @pl.when(is_next)
        def _():
            after = jnp.minimum(t + 1, TICKS - 1)

            @pl.when((t == 1) & moved)
            def _():
                wait_grad(2)

            for m in range(CHUNKS):
                @pl.when(t > 0)
                def _():
                    wait_sum(near, t, m, 1)

                total = product(t, m) + near[t, chunk(m)].astype(F32)

                @pl.when((t < TICKS - 1) & (apart | (t == 0)))
                def _():
                    first[after, chunk(m)] = total.astype(BF16)
                    first_copy(after, m).start()

                @pl.when((t > 0) & (t < TICKS - 1) & moved)
                def _():
                    res[after, half, chunk(m)] = (given(after, m) - total).astype(BF16)
                    res_copy(after, m).start()

                @pl.when(t == TICKS - 1)
                def _():
                    tail[m * group:(m + 1) * group] = laid(total)

            @pl.when((t == 0) & moved)
            def _():
                lay_blocks(0, per // 2)

            @pl.when((t == 1) & moved)
            def _():
                lay_blocks(per // 2, per)

            @pl.when((t > 0) & (t < TICKS - 1) & moved)
            def _():
                solve(after)

        @pl.when(jnp.logical_not(is_next))
        def _():
            for m in range(CHUNKS):
                @pl.when(t > 0)
                def _():
                    wait_sum(partial, t, m, 0)

                total = product(t, m) + partial[t, chunk(m)]

                @pl.when((t < TICKS - 1) & into_next)
                def _():
                    near_sums[t, chunk(m)] = total.astype(BF16)
                    near_sum(t, m).start()

                @pl.when((t < TICKS - 1) & jnp.logical_not(into_next))
                def _():
                    sums[t, chunk(m)] = total
                    far_sum(t, m).start()

                @pl.when(t == TICKS - 1)
                def _():
                    tail[m * group:(m + 1) * group] = laid(total)

    @pl.loop(0, TICKS)
    def _(t):
        @pl.when(is_next & moved & (t == TICKS - 1))
        def _():
            give_rest()

        @pl.when(is_lower & (blk >= t))
        def _():
            tick(t)

    has_tail = is_lower & (blk >= TICKS - 1)

    @pl.when(has_tail)
    def _():
        @pl.loop(0, owners)
        def _(o):
            give(o, tail.at[o], tail_in.at[slot], ts_sem, t_sem.at[slot])

    @pl.when(jnp.logical_not(is_upper))
    def _():
        wait_start()

    @pl.when(row > 0)
    def _():
        pltpu.make_async_copy(x_in.at[rest], x_in.at[rest], r_sem.at[1]).wait()

    @pl.loop(0, blocks)
    def _(s):
        t = row - s

        @pl.when((t >= 0) & (t < TICKS))
        def _():
            grad_own[s] = x_in[jnp.clip(t, 0, TICKS - 1)].astype(F32)[:rows]

        @pl.when(t >= TICKS)
        def _():
            ref = tail_in.at[jnp.minimum(s, tail_in.shape[0] - 1)]
            pltpu.make_async_copy(ref, ref, t_sem.at[jnp.minimum(s, tail_in.shape[0] - 1)]).wait()
            grad_own[s] = grad_own[s] - ref[...].astype(F32)[:rows]

    for p in range(blocks):
        out_ref[:, p * width:(p + 1) * width] = grad_own[starts_ref[p]]

    @pl.when(is_next & (blk == 0))
    def _():
        wait_grad(2)
        lay_blocks(per // 2, per)

    for k in range(3):
        @pl.when(((row > 0) | (k < 2)) & (col != pieces[k][2]))
        def _():
            grad_copy(k).wait_send()

    for h in range(2):
        @pl.when(is_diag & moved & (half == h))
        def _():
            for k in range(per):
                diag_copy(h, k).wait_send()

    @pl.when(is_lower)
    def _():
        tile_copy.wait_send()

    @pl.loop(0, TICKS)
    def _(t):
        for m in range(CHUNKS):
            @pl.when((row >= t) & ((is_diag & (apart | (t < 2))) | (is_next & moved & (t > 1))))
            def _():
                res_copy(t, m).wait_send()
                for k in range(2):
                    @pl.when(row + 1 + k < blocks)
                    def _():
                        solved_copy(t, m, k).wait_send()

            @pl.when(is_next & (row >= t) & ((t == 1) | (apart & (t > 0))))
            def _():
                first_copy(t, m).wait_send()

            @pl.when(is_lower & (blk >= t))
            def _():
                vec_copy(t, m).wait_send()

                @pl.when(row + 2 < blocks)
                def _():
                    forward_copy(t, m).wait_send()

                @pl.when((t < TICKS - 1) & into_next)
                def _():
                    near_sum(t, m).wait_send()

                @pl.when((t < TICKS - 1) & (row > blk + 2))
                def _():
                    far_sum(t, m).wait_send()

    def sent_all(ref_all, ref_less, sem):
        @pl.when(my_group == half)
        def _():
            pltpu.make_async_copy(ref_less, ref_less, sem).wait()

        @pl.when(my_group != half)
        def _():
            pltpu.make_async_copy(ref_all, ref_all, sem).wait()

    less = pl.ds(0, owners - 1)

    @pl.when(has_tail)
    def _():
        sent_all(tail, tail.at[less], ts_sem)

    @pl.when(is_diag)
    def _():
        sent_all(x_ret.at[start], x_ret.at[start, less], rs_sem.at[0])

    @pl.when((is_diag & apart & (row > 0)) | (is_next & moved))
    def _():
        sent_all(x_ret.at[rest], x_ret.at[rest, less], rs_sem.at[1])


def body(factor, gradient, starts):
    blocks = starts.shape[0]
    rows = gradient.shape[0]
    width = gradient.shape[1] // blocks
    tile_rows, half_rows = factor.shape
    owners = blocks
    vmem = pltpu.VMEM
    dma = pltpu.SemaphoreType.DMA
    spare = max(blocks - TICKS, 1)
    scratch = [
        vmem((2, half_rows, half_rows), BF16),
        vmem((tile_rows, half_rows), BF16),
        vmem((2, half_rows, half_rows), BF16),
        vmem((TICKS, 2, half_rows, width), BF16),
        vmem((TICKS, 2, half_rows, width), BF16),
        vmem((TICKS, half_rows, width), BF16),
        vmem((TICKS, half_rows, width), F32),
        vmem((TICKS, half_rows, width), F32),
        vmem((TICKS, half_rows, width), BF16),
        vmem((TICKS, half_rows, width), BF16),
        vmem((TICKS, half_rows, width), BF16),
        vmem((TICKS, half_rows, width), BF16),
        vmem((owners, 64, width), BF16),
        vmem((blocks, rows, width), F32),
        vmem((blocks, rows, width), F32),
        vmem((TICKS, 64, width), BF16),
        vmem((TICKS, owners, 64, width), BF16),
        vmem((TICKS, owners, 64, width), BF16),
        vmem((TICKS, 64, width), BF16),
        vmem((spare, 64, width), BF16),
        dma, dma((2,)), dma((half_rows // 128,)), dma((half_rows // 128,)), dma((3,)), dma((3,)),
        dma((2, TICKS, CHUNKS)), dma((2, TICKS, CHUNKS)), dma((2, TICKS, CHUNKS)),
        dma((TICKS, CHUNKS)), dma((TICKS, CHUNKS)), dma((2, TICKS, CHUNKS)), dma((2, TICKS, CHUNKS)),
        dma((TICKS, CHUNKS)), dma((TICKS, CHUNKS)), dma((2,)), dma((2,)), dma, dma((spare,)),
    ]
    return pl.pallas_call(
        functools.partial(kernel, blocks),
        out_shape=jax.ShapeDtypeStruct(gradient.shape, F32),
        in_specs=[
            pl.BlockSpec(memory_space=pltpu.SMEM),
            pl.BlockSpec(memory_space=pltpu.VMEM),
            pl.BlockSpec(memory_space=pl.ANY),
        ],
        out_specs=pl.BlockSpec(memory_space=pltpu.VMEM),
        scratch_shapes=scratch,
        compiler_params=pltpu.CompilerParams(
            collective_id=0, has_side_effects=True, vmem_limit_bytes=62 * 1024 * 1024
        ),
        cost_estimate=pl.CostEstimate(
            flops=2 * TICKS * tile_rows * half_rows * width,
            bytes_accessed=2 * tile_rows * half_rows, transcendentals=0,
        ),
    )(starts, gradient, factor)


def solution(mesh):
    in_specs = (P("row", "col"), P(("row", "col"), None), P())
    out_specs = P(("row", "col"), None)
    return jax.shard_map(body, mesh=mesh, in_specs=in_specs, out_specs=out_specs, check_vma=False)
```

```python
import functools
import jax
import jax.numpy as jnp
from jax import lax
from jax.experimental import pallas as pl
from jax.experimental.pallas import tpu as pltpu
from jax.sharding import PartitionSpec as P

TICKS = 6
CHUNKS = 4
FIRST = 3
SINGLE = 3
EARLY = 3
MESH = pl.DeviceIdType.MESH
F32 = jnp.float32
BF16 = jnp.bfloat16


def kernel(
    blocks, starts_ref, grad_ref, factor_ref, out_ref,
    tile, raw, diag, vec, res, solved, partial, sums, near, near_sums, first, first_in,
    tail, grad_all, grad_given, grad_own, grad_send, grad_in, x_ret, x_in, tail_in,
    grad_sem, load_sem, tile_sem, us_sem, u_sem, gs_sem, g_sem, vs_sem, v_sem, xs_sem, qs_sem, q_sem,
    ss_sem, s_sem, fs_sem, f_sem, rs_sem, r_sem, ts_sem, t_sem,
):
    row = lax.axis_index("row")
    col = lax.axis_index("col")
    blk = col // 2
    half = col % 2
    owners = blocks
    rows = grad_ref.shape[0]
    width = grad_ref.shape[1] // blocks
    half_rows = factor_ref.shape[1]
    step = half_rows // CHUNKS
    group = owners // CHUNKS
    lanes = 128
    per = half_rows // lanes
    sib = col + 1 - 2 * half
    other = 1 - half
    is_diag = row == blk
    is_next = row == blk + 1
    is_lower = row > blk
    limit = jnp.where(row % 4 == 0, TICKS, FIRST)
    moved = (row >= limit) & (limit < TICKS)
    my_group = col // owners
    diag_core = 2 * row + my_group
    next_core = jnp.where(row > 0, diag_core - 2, diag_core)

    own_rows = pl.ds(pl.multiple_of(half * half_rows, half_rows), half_rows)
    other_rows = pl.ds(pl.multiple_of(other * half_rows, half_rows), half_rows)
    load_raw = pltpu.make_async_copy(factor_ref, raw, load_sem)
    load_half = pltpu.make_async_copy(factor_ref.at[own_rows], tile.at[half], load_sem)

    load_grad = pltpu.make_async_copy(grad_ref, grad_all, grad_sem)
    load_grad.start()

    @pl.when(is_diag)
    def _():
        load_raw.start()

    @pl.when(is_lower)
    def _():
        load_half.start()

    barrier = pltpu.get_barrier_semaphore()

    @pl.loop(0, 2 * blocks)
    def _(c):
        @pl.when(c != col)
        def _():
            pl.semaphore_signal(barrier, inc=1, device_id=(row, c), device_id_type=MESH)

    far = [(1, 0), (2, 0), (-1, 0), (-2, 0), (1, 2), (2, 2), (-1, -2), (-2, -2)]
    for dr, dc in far:
        pl.semaphore_signal(
            barrier, inc=1, device_id=((row + dr + blocks) % blocks, (col + dc + 2 * blocks) % (2 * blocks)),
            device_id_type=MESH,
        )

    load_grad.wait()
    for p in range(blocks):
        grad_given[p] = grad_all[:, p * width:(p + 1) * width]
    for s in range(blocks):
        which = jnp.int32(0)
        for p in range(blocks):
            which = which + jnp.where(starts_ref[p] == s, p, 0)
        grad_own[s] = grad_given[jnp.minimum(which, blocks - 1)]
    pad = jnp.zeros((64 - rows, width), F32)

    @pl.loop(0, TICKS)
    def _(t):
        @pl.when(row >= t)
        def _():
            grad_send[t] = jnp.concatenate([grad_own[row - t], pad], axis=0).astype(BF16)

        @pl.when(row < t)
        def _():
            grad_send[t] = jnp.zeros((64, width), BF16)

    pl.semaphore_wait(barrier, 2 * blocks - 1 + len(far))

    my_slot = col % owners

    def grad_target(t):
        return jnp.where(t < limit, diag_core, next_core)

    def grad_copy(t):
        return pltpu.make_async_remote_copy(
            src_ref=grad_send.at[t], dst_ref=grad_in.at[t, my_slot],
            send_sem=gs_sem.at[t], recv_sem=g_sem.at[t],
            device_id=(row, grad_target(t)), device_id_type=MESH,
        )

    def wait_grad(t):
        pltpu.make_async_copy(grad_in.at[t], grad_in.at[t], g_sem.at[t]).wait()

    def send_grad(t):
        @pl.when((row >= t) & (col != grad_target(t)))
        def _():
            grad_copy(t).start()

        @pl.when((row >= t) & (col == grad_target(t)))
        def _():
            pltpu.make_async_copy(grad_send.at[t], grad_in.at[t, my_slot], g_sem.at[t]).start()

    def sent_grad(t):
        @pl.when((row >= t) & (col != grad_target(t)))
        def _():
            grad_copy(t).wait_send()

    send_grad(0)

    def diag_copy(h, k):
        part = (pl.ds(0, h * half_rows + (k + 1) * lanes), pl.ds(k * lanes, lanes))
        return pltpu.make_async_remote_copy(
            src_ref=factor_ref.at[part], dst_ref=raw.at[part],
            send_sem=us_sem.at[k], recv_sem=u_sem.at[k],
            device_id=(row, (col - 2 + 2 * blocks) % (2 * blocks)), device_id_type=MESH,
        )

    for h in range(2):
        @pl.when(is_diag & moved & (half == h))
        def _():
            for k in range(per):
                diag_copy(h, k).start()

    tile_copy = pltpu.make_async_remote_copy(
        src_ref=factor_ref.at[other_rows], dst_ref=tile.at[half],
        send_sem=tile_sem.at[0], recv_sem=tile_sem.at[1],
        device_id=(row, sib), device_id_type=MESH,
    )

    @pl.when(is_lower)
    def _():
        tile_copy.start()

    def lay_diag(k):
        m = slice(k * lanes, (k + 1) * lanes)

        @pl.loop(0, 2 * per)
        def _(n):
            src = pl.ds(pl.multiple_of(n * lanes, lanes), lanes)
            dst = pl.ds(pl.multiple_of((n % per) * lanes, lanes), lanes)

            @pl.when(n <= half * per + k)
            def _():
                diag[n // per, m, dst] = raw[src, m].T

            @pl.when(n > half * per + k)
            def _():
                diag[n // per, m, dst] = jnp.zeros((lanes, lanes), BF16)

    def chunk(m):
        return pl.ds(pl.multiple_of(m * step, step), step)

    def sibling_copy(ref, t, m, send_sem, recv_sem):
        part = ref.at[t, half, chunk(m)]
        return pltpu.make_async_remote_copy(
            src_ref=part, dst_ref=part, send_sem=send_sem.at[t, m], recv_sem=recv_sem.at[t, m],
            device_id=(row, sib), device_id_type=MESH,
        )

    def vec_copy(t, m):
        return sibling_copy(vec, t, m, vs_sem.at[0], v_sem.at[0])

    def res_copy(t, m):
        return sibling_copy(res, t, m, qs_sem, q_sem)

    def forward_copy(t, m):
        part = vec.at[t, half, chunk(m)]
        return pltpu.make_async_remote_copy(
            src_ref=part, dst_ref=part, send_sem=vs_sem.at[1, t, m], recv_sem=v_sem.at[1, t, m],
            device_id=((row + 2) % blocks, col), device_id_type=MESH,
        )

    def solved_copy(t, m, k):
        return pltpu.make_async_remote_copy(
            src_ref=solved.at[t, chunk(m)], dst_ref=vec.at[t, half, chunk(m)],
            send_sem=xs_sem.at[k, t, m], recv_sem=v_sem.at[1, t, m],
            device_id=((row + 1 + k) % blocks, 2 * row + half), device_id_type=MESH,
        )

    into_next = row == blk + 2
    right = (row, (col + 2) % (2 * blocks))

    def partial_copy(t, m, src, dst, k):
        return pltpu.make_async_remote_copy(
            src_ref=src.at[t, chunk(m)], dst_ref=dst.at[(t + 1) % TICKS, chunk(m)],
            send_sem=ss_sem.at[k, t, m], recv_sem=s_sem.at[k, (t + 1) % TICKS, m],
            device_id=right, device_id_type=MESH,
        )

    def far_sum(t, m):
        return partial_copy(t, m, sums, partial, 0)

    def near_sum(t, m):
        return partial_copy(t, m, near_sums, near, 1)

    def wait_sum(ref, t, m, k):
        pltpu.make_async_copy(ref.at[t, chunk(m)], ref.at[t, chunk(m)], s_sem.at[k, t, m]).wait()

    def first_copy(t, m):
        return pltpu.make_async_remote_copy(
            src_ref=first.at[t, chunk(m)], dst_ref=first_in.at[t, chunk(m)],
            send_sem=fs_sem.at[t, m], recv_sem=f_sem.at[t, m], device_id=right, device_id_type=MESH,
        )

    padding = jnp.zeros((group, 64 - rows, width), F32)

    def laid(y):
        return jnp.concatenate([y.reshape(group, rows, width), padding], axis=1).astype(BF16)

    def given(t, m):
        return grad_in[t, m * group:(m + 1) * group].astype(F32)[:, :rows].reshape(step, width)

    def give(o, src, dst, send_sem, recv_sem):
        target = half * owners + o

        @pl.when(target != col)
        def _():
            pltpu.make_async_remote_copy(
                src_ref=src, dst_ref=dst, send_sem=send_sem, recv_sem=recv_sem,
                device_id=(row, target), device_id_type=MESH,
            ).start()

        @pl.when(target == col)
        def _():
            pltpu.make_async_copy(src, dst, recv_sem).start()

    slot = jnp.clip(blk - (TICKS - 1), 0, tail_in.shape[0] - 1)

    def solve(t):
        for m in range(CHUNKS):
            res_copy(t, m).wait_recv()
        for m in range(CHUNKS):
            x = jnp.dot(diag[0, chunk(m)], res[t, 0], preferred_element_type=F32)
            x = x + jnp.dot(diag[1, chunk(m)], res[t, 1], preferred_element_type=F32)
            solved[t, chunk(m)] = x.astype(BF16)
            x_ret[t, m * group:(m + 1) * group] = laid(x)

            @pl.when(row + 1 < blocks)
            def _():
                solved_copy(t, m, 0).start()

        @pl.when(row + 2 < blocks)
        def _():
            for m in range(CHUNKS):
                solved_copy(t, m, 1).start()

        @pl.when(t < SINGLE)
        def _():
            @pl.loop(0, owners)
            def _(o):
                give(o, x_ret.at[t, o], x_in.at[t], rs_sem.at[t], r_sem.at[t])

    rest = pl.ds(SINGLE, TICKS - SINGLE)
    rest_by_diag = limit == TICKS

    def give_rest():
        @pl.loop(0, owners)
        def _(o):
            give(o, x_ret.at[rest, o], x_in.at[rest], rs_sem.at[SINGLE], r_sem.at[SINGLE])

    def solve_apart(t):
        for m in range(CHUNKS):
            first_copy(t, m).wait_recv()
            res[t, half, chunk(m)] = (given(t, m) - first_in[t, chunk(m)].astype(F32)).astype(BF16)
            res_copy(t, m).start()
        solve(t)

    @pl.when(is_diag)
    def _():
        load_raw.wait()
        for k in range(per):
            lay_diag(k)

    sent_grad(0)
    send_grad(1)
    sent_grad(1)
    for t in range(2, EARLY):
        send_grad(t)

    def send_late():
        for t in range(EARLY, TICKS):
            send_grad(t)

    @pl.when(is_diag)
    def _():
        wait_grad(0)
        for m in range(CHUNKS):
            res[0, half, chunk(m)] = given(0, m).astype(BF16)
            res_copy(0, m).start()
        solve(0)
        send_late()

        @pl.loop(1, TICKS)
        def _(t):
            @pl.when((row >= t) & (t < limit))
            def _():
                wait_grad(t)
                solve_apart(t)

        @pl.when(rest_by_diag & (row >= SINGLE))
        def _():
            give_rest()

    @pl.when(is_lower)
    def _():
        partial[0] = jnp.zeros_like(partial[0])
        near[0] = jnp.zeros_like(near[0])
        load_half.wait()
        tile_copy.wait_recv()

    def lay_blocks(lo, hi):
        for k in range(lo, hi):
            for h in range(2):
                @pl.when(half == h)
                def _():
                    diag_copy(h, k).wait_recv()
            lay_diag(k)

    def product(t, m):
        y = jnp.dot(tile[0, chunk(m)], vec[t, 0], preferred_element_type=F32)
        return y + jnp.dot(tile[1, chunk(m)], vec[t, 1], preferred_element_type=F32)

    def tick(t):
        for m in range(CHUNKS):
            forward_copy(t, m).wait_recv()

            @pl.when(row + 2 < blocks)
            def _():
                forward_copy(t, m).start()

            vec_copy(t, m).start()

        for m in range(CHUNKS):
            vec_copy(t, m).wait_recv()

        @pl.when(is_next)
        def _():
            after = jnp.minimum(t + 1, TICKS - 1)

            fused = (t + 1 >= limit) & (t < TICKS - 1)

            @pl.when(fused)
            def _():
                wait_grad(after)

            for m in range(CHUNKS):
                @pl.when(t > 0)
                def _():
                    wait_sum(near, t, m, 1)

                total = product(t, m) + near[t, chunk(m)].astype(F32)

                @pl.when(t + 1 < limit)
                def _():
                    first[after, chunk(m)] = total.astype(BF16)
                    first_copy(after, m).start()

                @pl.when(fused)
                def _():
                    res[after, half, chunk(m)] = (given(after, m) - total).astype(BF16)
                    res_copy(after, m).start()

                @pl.when(t == TICKS - 1)
                def _():
                    tail[m * group:(m + 1) * group] = laid(total)

            @pl.when((t == limit - 2) & moved)
            def _():
                lay_blocks(0, per // 2)

            @pl.when((t == limit - 1) & moved)
            def _():
                lay_blocks(per // 2, per)

            @pl.when(fused)
            def _():
                solve(after)

        @pl.when(jnp.logical_not(is_next))
        def _():
            for m in range(CHUNKS):
                @pl.when(t > 0)
                def _():
                    wait_sum(partial, t, m, 0)

                total = product(t, m) + partial[t, chunk(m)]

                @pl.when((t < TICKS - 1) & into_next)
                def _():
                    near_sums[t, chunk(m)] = total.astype(BF16)
                    near_sum(t, m).start()

                @pl.when((t < TICKS - 1) & jnp.logical_not(into_next))
                def _():
                    sums[t, chunk(m)] = total
                    far_sum(t, m).start()

                @pl.when(t == TICKS - 1)
                def _():
                    tail[m * group:(m + 1) * group] = laid(total)

    def wait_solved(t):
        pltpu.make_async_copy(x_in.at[t], x_in.at[t], r_sem.at[t]).wait()

    @pl.when(row < blk)
    def _():
        wait_solved(0)
        send_late()

    @pl.loop(0, TICKS)
    def _(t):
        @pl.when(is_lower & (t == 1))
        def _():
            send_late()

        @pl.when(is_next & (t == TICKS - 1) & (row >= SINGLE) & jnp.logical_not(rest_by_diag))
        def _():
            give_rest()

        @pl.when(is_lower & (blk >= t))
        def _():
            tick(t)

    has_tail = is_lower & (blk >= TICKS - 1)

    @pl.when(has_tail)
    def _():
        @pl.loop(0, owners)
        def _(o):
            give(o, tail.at[o], tail_in.at[slot], ts_sem, t_sem.at[slot])

    @pl.loop(0, SINGLE)
    def _(t):
        @pl.when((row >= t) & ((t > 0) | (row >= blk)))
        def _():
            wait_solved(t)

    @pl.when(row >= SINGLE)
    def _():
        pltpu.make_async_copy(x_in.at[rest], x_in.at[rest], r_sem.at[SINGLE]).wait()

    @pl.loop(0, blocks)
    def _(s):
        t = row - s

        @pl.when((t >= 0) & (t < TICKS))
        def _():
            grad_own[s] = x_in[jnp.clip(t, 0, TICKS - 1)].astype(F32)[:rows]

        @pl.when(t >= TICKS)
        def _():
            ref = tail_in.at[jnp.minimum(s, tail_in.shape[0] - 1)]
            pltpu.make_async_copy(ref, ref, t_sem.at[jnp.minimum(s, tail_in.shape[0] - 1)]).wait()
            grad_own[s] = grad_own[s] - ref[...].astype(F32)[:rows]

    for p in range(blocks):
        out_ref[:, p * width:(p + 1) * width] = grad_own[starts_ref[p]]

    for t in range(2, TICKS):
        sent_grad(t)

    for h in range(2):
        @pl.when(is_diag & moved & (half == h))
        def _():
            for k in range(per):
                diag_copy(h, k).wait_send()

    @pl.when(is_lower)
    def _():
        tile_copy.wait_send()

    @pl.loop(0, TICKS)
    def _(t):
        for m in range(CHUNKS):
            @pl.when((row >= t) & ((is_diag & (t < limit)) | (is_next & (t >= limit))))
            def _():
                res_copy(t, m).wait_send()
                for k in range(2):
                    @pl.when(row + 1 + k < blocks)
                    def _():
                        solved_copy(t, m, k).wait_send()

            @pl.when(is_next & (row >= t) & (t > 0) & (t < limit))
            def _():
                first_copy(t, m).wait_send()

            @pl.when(is_lower & (blk >= t))
            def _():
                vec_copy(t, m).wait_send()

                @pl.when(row + 2 < blocks)
                def _():
                    forward_copy(t, m).wait_send()

                @pl.when((t < TICKS - 1) & into_next)
                def _():
                    near_sum(t, m).wait_send()

                @pl.when((t < TICKS - 1) & (row > blk + 2))
                def _():
                    far_sum(t, m).wait_send()

    def sent_all(ref_all, ref_less, sem):
        @pl.when(my_group == half)
        def _():
            pltpu.make_async_copy(ref_less, ref_less, sem).wait()

        @pl.when(my_group != half)
        def _():
            pltpu.make_async_copy(ref_all, ref_all, sem).wait()

    less = pl.ds(0, owners - 1)

    @pl.when(has_tail)
    def _():
        sent_all(tail, tail.at[less], ts_sem)

    @pl.loop(0, SINGLE)
    def _(t):
        @pl.when((row >= t) & ((is_diag & (t < limit)) | (is_next & (t >= limit))))
        def _():
            sent_all(x_ret.at[t], x_ret.at[t, less], rs_sem.at[t])

    @pl.when((row >= SINGLE) & ((is_diag & rest_by_diag) | (is_next & jnp.logical_not(rest_by_diag))))
    def _():
        sent_all(x_ret.at[rest], x_ret.at[rest, less], rs_sem.at[SINGLE])


def body(factor, gradient, starts):
    blocks = starts.shape[0]
    rows = gradient.shape[0]
    width = gradient.shape[1] // blocks
    tile_rows, half_rows = factor.shape
    owners = blocks
    vmem = pltpu.VMEM
    dma = pltpu.SemaphoreType.DMA
    spare = max(blocks - TICKS, 1)
    scratch = [
        vmem((2, half_rows, half_rows), BF16),
        vmem((tile_rows, half_rows), BF16),
        vmem((2, half_rows, half_rows), BF16),
        vmem((TICKS, 2, half_rows, width), BF16),
        vmem((TICKS, 2, half_rows, width), BF16),
        vmem((TICKS, half_rows, width), BF16),
        vmem((TICKS, half_rows, width), F32),
        vmem((TICKS, half_rows, width), F32),
        vmem((TICKS, half_rows, width), BF16),
        vmem((TICKS, half_rows, width), BF16),
        vmem((TICKS, half_rows, width), BF16),
        vmem((TICKS, half_rows, width), BF16),
        vmem((owners, 64, width), BF16),
        vmem(gradient.shape, F32),
        vmem((blocks, rows, width), F32),
        vmem((blocks, rows, width), F32),
        vmem((TICKS, 64, width), BF16),
        vmem((TICKS, owners, 64, width), BF16),
        vmem((TICKS, owners, 64, width), BF16),
        vmem((TICKS, 64, width), BF16),
        vmem((spare, 64, width), BF16),
        dma, dma, dma((2,)), dma((half_rows // 128,)), dma((half_rows // 128,)), dma((TICKS,)), dma((TICKS,)),
        dma((2, TICKS, CHUNKS)), dma((2, TICKS, CHUNKS)), dma((2, TICKS, CHUNKS)),
        dma((TICKS, CHUNKS)), dma((TICKS, CHUNKS)), dma((2, TICKS, CHUNKS)), dma((2, TICKS, CHUNKS)),
        dma((TICKS, CHUNKS)), dma((TICKS, CHUNKS)), dma((TICKS,)), dma((TICKS,)), dma, dma((spare,)),
    ]
    return pl.pallas_call(
        functools.partial(kernel, blocks),
        out_shape=jax.ShapeDtypeStruct(gradient.shape, F32),
        in_specs=[
            pl.BlockSpec(memory_space=pltpu.SMEM),
            pl.BlockSpec(memory_space=pl.ANY),
            pl.BlockSpec(memory_space=pl.ANY),
        ],
        out_specs=pl.BlockSpec(memory_space=pltpu.VMEM),
        scratch_shapes=scratch,
        compiler_params=pltpu.CompilerParams(
            collective_id=0, has_side_effects=True, vmem_limit_bytes=62 * 1024 * 1024
        ),
        cost_estimate=pl.CostEstimate(
            flops=2 * TICKS * tile_rows * half_rows * width,
            bytes_accessed=2 * tile_rows * half_rows, transcendentals=0,
        ),
    )(starts, gradient, factor)


def solution(mesh):
    in_specs = (P("row", "col"), P(("row", "col"), None), P())
    out_specs = P(("row", "col"), None)
    return jax.shard_map(body, mesh=mesh, in_specs=in_specs, out_specs=out_specs, check_vma=False)
```

```python
import functools
import jax
import jax.numpy as jnp
from jax import lax
from jax.experimental import pallas as pl
from jax.experimental.pallas import tpu as pltpu
from jax.sharding import PartitionSpec as P

TICKS = 6
CHUNKS = 4
FIRST = 3
SINGLE = 3
EARLY = 3
MESH = pl.DeviceIdType.MESH
F32 = jnp.float32
BF16 = jnp.bfloat16


def kernel(
    blocks, starts_ref, grad_ref, factor_ref, out_ref,
    tile, raw, diag, vec, res, solved, partial, sums, near, near_sums, first, first_in,
    own_part, tail, grad_all, grad_given, grad_own, grad_send, grad_in, x_ret, x_in, tail_in,
    grad_sem, load_sem, tile_sem, us_sem, u_sem, gs_sem, g_sem, vs_sem, v_sem, xs_sem, qs_sem, q_sem,
    ss_sem, s_sem, fs_sem, f_sem, rs_sem, r_sem, ts_sem, t_sem,
):
    row = lax.axis_index("row")
    col = lax.axis_index("col")
    blk = col // 2
    half = col % 2
    owners = blocks
    rows = grad_ref.shape[0]
    width = grad_ref.shape[1] // blocks
    half_rows = factor_ref.shape[1]
    step = half_rows // CHUNKS
    group = owners // CHUNKS
    lanes = 128
    per = half_rows // lanes
    sib = col + 1 - 2 * half
    other = 1 - half
    is_diag = row == blk
    is_next = row == blk + 1
    is_lower = row > blk
    limit = jnp.where(row % 4 == 0, TICKS, FIRST)
    moved = (row >= limit) & (limit < TICKS)
    my_group = col // owners
    diag_core = 2 * row + my_group
    next_core = jnp.where(row > 0, diag_core - 2, diag_core)

    own_rows = pl.ds(pl.multiple_of(half * half_rows, half_rows), half_rows)
    other_rows = pl.ds(pl.multiple_of(other * half_rows, half_rows), half_rows)
    load_raw = pltpu.make_async_copy(factor_ref, raw, load_sem)
    load_half = pltpu.make_async_copy(factor_ref.at[own_rows], tile.at[half], load_sem)

    load_grad = pltpu.make_async_copy(grad_ref, grad_all, grad_sem)
    load_grad.start()

    @pl.when(is_diag)
    def _():
        load_raw.start()

    @pl.when(is_lower)
    def _():
        load_half.start()

    barrier = pltpu.get_barrier_semaphore()

    @pl.loop(0, 2 * blocks)
    def _(c):
        @pl.when(c != col)
        def _():
            pl.semaphore_signal(barrier, inc=1, device_id=(row, c), device_id_type=MESH)

    far = [(1, 0), (2, 0), (-1, 0), (-2, 0), (1, 2), (2, 2), (-1, -2), (-2, -2)]
    for dr, dc in far:
        pl.semaphore_signal(
            barrier, inc=1, device_id=((row + dr + blocks) % blocks, (col + dc + 2 * blocks) % (2 * blocks)),
            device_id_type=MESH,
        )

    load_grad.wait()
    for p in range(blocks):
        grad_given[p] = grad_all[:, p * width:(p + 1) * width]
    for s in range(blocks):
        which = jnp.int32(0)
        for p in range(blocks):
            which = which + jnp.where(starts_ref[p] == s, p, 0)
        grad_own[s] = grad_given[jnp.minimum(which, blocks - 1)]
    pad = jnp.zeros((64 - rows, width), F32)

    @pl.loop(0, TICKS)
    def _(t):
        @pl.when(row >= t)
        def _():
            grad_send[t] = jnp.concatenate([grad_own[row - t], pad], axis=0).astype(BF16)

        @pl.when(row < t)
        def _():
            grad_send[t] = jnp.zeros((64, width), BF16)

    pl.semaphore_wait(barrier, 2 * blocks - 1 + len(far))

    my_slot = col % owners

    def grad_target(t):
        return jnp.where(t < limit, diag_core, next_core)

    def grad_copy(t):
        return pltpu.make_async_remote_copy(
            src_ref=grad_send.at[t], dst_ref=grad_in.at[t, my_slot],
            send_sem=gs_sem.at[t], recv_sem=g_sem.at[t],
            device_id=(row, grad_target(t)), device_id_type=MESH,
        )

    def wait_grad(t):
        pltpu.make_async_copy(grad_in.at[t], grad_in.at[t], g_sem.at[t]).wait()

    def send_grad(t):
        @pl.when((row >= t) & (col != grad_target(t)))
        def _():
            grad_copy(t).start()

        @pl.when((row >= t) & (col == grad_target(t)))
        def _():
            pltpu.make_async_copy(grad_send.at[t], grad_in.at[t, my_slot], g_sem.at[t]).start()

    def sent_grad(t):
        @pl.when((row >= t) & (col != grad_target(t)))
        def _():
            grad_copy(t).wait_send()

    send_grad(0)

    def diag_copy(h, k):
        part = (pl.ds(0, h * half_rows + (k + 1) * lanes), pl.ds(k * lanes, lanes))
        return pltpu.make_async_remote_copy(
            src_ref=factor_ref.at[part], dst_ref=raw.at[part],
            send_sem=us_sem.at[k], recv_sem=u_sem.at[k],
            device_id=(row, (col - 2 + 2 * blocks) % (2 * blocks)), device_id_type=MESH,
        )

    for h in range(2):
        @pl.when(is_diag & moved & (half == h))
        def _():
            for k in range(per):
                diag_copy(h, k).start()

    tile_copy = pltpu.make_async_remote_copy(
        src_ref=factor_ref.at[other_rows], dst_ref=tile.at[half],
        send_sem=tile_sem.at[0], recv_sem=tile_sem.at[1],
        device_id=(row, sib), device_id_type=MESH,
    )

    @pl.when(is_lower)
    def _():
        tile_copy.start()

    def lay_diag(k):
        m = slice(k * lanes, (k + 1) * lanes)

        @pl.loop(0, 2 * per)
        def _(n):
            src = pl.ds(pl.multiple_of(n * lanes, lanes), lanes)
            dst = pl.ds(pl.multiple_of((n % per) * lanes, lanes), lanes)

            @pl.when(n <= half * per + k)
            def _():
                diag[n // per, m, dst] = raw[src, m].T

            @pl.when(n > half * per + k)
            def _():
                diag[n // per, m, dst] = jnp.zeros((lanes, lanes), BF16)

    def chunk(m):
        return pl.ds(pl.multiple_of(m * step, step), step)

    def sibling_copy(ref, t, m, send_sem, recv_sem):
        part = ref.at[t, half, chunk(m)]
        return pltpu.make_async_remote_copy(
            src_ref=part, dst_ref=part, send_sem=send_sem.at[t, m], recv_sem=recv_sem.at[t, m],
            device_id=(row, sib), device_id_type=MESH,
        )

    def vec_copy(t, m):
        return sibling_copy(vec, t, m, vs_sem.at[0], v_sem.at[0])

    def res_copy(t, m):
        return sibling_copy(res, t, m, qs_sem, q_sem)

    def forward_copy(t, m):
        part = vec.at[t, half, chunk(m)]
        return pltpu.make_async_remote_copy(
            src_ref=part, dst_ref=part, send_sem=vs_sem.at[1, t, m], recv_sem=v_sem.at[1, t, m],
            device_id=((row + 2) % blocks, col), device_id_type=MESH,
        )

    def solved_copy(t, m, k):
        return pltpu.make_async_remote_copy(
            src_ref=solved.at[t, chunk(m)], dst_ref=vec.at[t, half, chunk(m)],
            send_sem=xs_sem.at[k, t, m], recv_sem=v_sem.at[1, t, m],
            device_id=((row + 1 + k) % blocks, 2 * row + half), device_id_type=MESH,
        )

    into_next = row == blk + 2
    right = (row, (col + 2) % (2 * blocks))

    def partial_copy(t, m, src, dst, k):
        return pltpu.make_async_remote_copy(
            src_ref=src.at[t, chunk(m)], dst_ref=dst.at[(t + 1) % TICKS, chunk(m)],
            send_sem=ss_sem.at[k, t, m], recv_sem=s_sem.at[k, (t + 1) % TICKS, m],
            device_id=right, device_id_type=MESH,
        )

    def far_sum(t, m):
        return partial_copy(t, m, sums, partial, 0)

    def near_sum(t, m):
        return partial_copy(t, m, near_sums, near, 1)

    def wait_sum(ref, t, m, k):
        pltpu.make_async_copy(ref.at[t, chunk(m)], ref.at[t, chunk(m)], s_sem.at[k, t, m]).wait()

    def first_copy(t, m):
        return pltpu.make_async_remote_copy(
            src_ref=first.at[t, chunk(m)], dst_ref=first_in.at[t, chunk(m)],
            send_sem=fs_sem.at[t, m], recv_sem=f_sem.at[t, m], device_id=right, device_id_type=MESH,
        )

    padding = jnp.zeros((group, 64 - rows, width), F32)

    def laid(y):
        return jnp.concatenate([y.reshape(group, rows, width), padding], axis=1).astype(BF16)

    def given(t, m):
        return grad_in[t, m * group:(m + 1) * group].astype(F32)[:, :rows].reshape(step, width)

    def give(o, src, dst, send_sem, recv_sem):
        target = half * owners + o

        @pl.when(target != col)
        def _():
            pltpu.make_async_remote_copy(
                src_ref=src, dst_ref=dst, send_sem=send_sem, recv_sem=recv_sem,
                device_id=(row, target), device_id_type=MESH,
            ).start()

        @pl.when(target == col)
        def _():
            pltpu.make_async_copy(src, dst, recv_sem).start()

    slot = jnp.clip(blk - (TICKS - 1), 0, tail_in.shape[0] - 1)

    def solve(t):
        for m in range(CHUNKS):
            own_part[chunk(m)] = jnp.dot(diag[half, chunk(m)], res[t, half], preferred_element_type=F32)
        for m in range(CHUNKS):
            res_copy(t, m).wait_recv()
        for m in range(CHUNKS):
            x = own_part[chunk(m)] + jnp.dot(diag[other, chunk(m)], res[t, other], preferred_element_type=F32)
            solved[t, chunk(m)] = x.astype(BF16)

            @pl.when(row + 1 < blocks)
            def _():
                solved_copy(t, m, 0).start()

            x_ret[t, m * group:(m + 1) * group] = laid(x)

        @pl.when(row + 2 < blocks)
        def _():
            for m in range(CHUNKS):
                solved_copy(t, m, 1).start()

        @pl.when(t < SINGLE)
        def _():
            @pl.loop(0, owners)
            def _(o):
                give(o, x_ret.at[t, o], x_in.at[t], rs_sem.at[t], r_sem.at[t])

    rest = pl.ds(SINGLE, TICKS - SINGLE)
    rest_by_diag = limit == TICKS

    def give_rest():
        @pl.loop(0, owners)
        def _(o):
            give(o, x_ret.at[rest, o], x_in.at[rest], rs_sem.at[SINGLE], r_sem.at[SINGLE])

    def solve_apart(t):
        for m in range(CHUNKS):
            first_copy(t, m).wait_recv()
            res[t, half, chunk(m)] = (given(t, m) - first_in[t, chunk(m)].astype(F32)).astype(BF16)
            res_copy(t, m).start()
        solve(t)

    @pl.when(is_diag)
    def _():
        load_raw.wait()
        for k in range(per):
            lay_diag(k)

    sent_grad(0)
    send_grad(1)
    sent_grad(1)
    for t in range(2, EARLY):
        send_grad(t)

    def send_late():
        for t in range(EARLY, TICKS):
            send_grad(t)

    @pl.when(is_diag)
    def _():
        wait_grad(0)
        for m in range(CHUNKS):
            res[0, half, chunk(m)] = given(0, m).astype(BF16)
            res_copy(0, m).start()
        solve(0)
        send_late()

        @pl.loop(1, TICKS)
        def _(t):
            @pl.when((row >= t) & (t < limit))
            def _():
                wait_grad(t)
                solve_apart(t)

        @pl.when(rest_by_diag & (row >= SINGLE))
        def _():
            give_rest()

    @pl.when(is_lower)
    def _():
        partial[0] = jnp.zeros_like(partial[0])
        near[0] = jnp.zeros_like(near[0])
        load_half.wait()
        tile_copy.wait_recv()

    def lay_blocks(lo, hi):
        for k in range(lo, hi):
            for h in range(2):
                @pl.when(half == h)
                def _():
                    diag_copy(h, k).wait_recv()
            lay_diag(k)

    def product(t, m):
        return own_part[chunk(m)] + jnp.dot(tile[other, chunk(m)], vec[t, other], preferred_element_type=F32)

    def tick(t):
        for m in range(CHUNKS):
            forward_copy(t, m).wait_recv()

            vec_copy(t, m).start()

            @pl.when(row + 2 < blocks)
            def _():
                forward_copy(t, m).start()

        for m in range(CHUNKS):
            own_part[chunk(m)] = jnp.dot(tile[half, chunk(m)], vec[t, half], preferred_element_type=F32)

        for m in range(CHUNKS):
            vec_copy(t, m).wait_recv()

        @pl.when(is_next)
        def _():
            after = jnp.minimum(t + 1, TICKS - 1)

            fused = (t + 1 >= limit) & (t < TICKS - 1)

            @pl.when(fused)
            def _():
                wait_grad(after)

            for m in range(CHUNKS):
                @pl.when(t > 0)
                def _():
                    wait_sum(near, t, m, 1)

                total = product(t, m) + near[t, chunk(m)].astype(F32)

                @pl.when(t + 1 < limit)
                def _():
                    first[after, chunk(m)] = total.astype(BF16)
                    first_copy(after, m).start()

                @pl.when(fused)
                def _():
                    res[after, half, chunk(m)] = (given(after, m) - total).astype(BF16)
                    res_copy(after, m).start()

                @pl.when(t == TICKS - 1)
                def _():
                    tail[m * group:(m + 1) * group] = laid(total)

            @pl.when((t == limit - 2) & moved)
            def _():
                lay_blocks(0, per // 2)

            @pl.when((t == limit - 1) & moved)
            def _():
                lay_blocks(per // 2, per)

            @pl.when(fused)
            def _():
                solve(after)

        @pl.when(jnp.logical_not(is_next))
        def _():
            for m in range(CHUNKS):
                @pl.when(t > 0)
                def _():
                    wait_sum(partial, t, m, 0)

                total = product(t, m) + partial[t, chunk(m)]

                @pl.when((t < TICKS - 1) & into_next)
                def _():
                    near_sums[t, chunk(m)] = total.astype(BF16)
                    near_sum(t, m).start()

                @pl.when((t < TICKS - 1) & jnp.logical_not(into_next))
                def _():
                    sums[t, chunk(m)] = total
                    far_sum(t, m).start()

                @pl.when(t == TICKS - 1)
                def _():
                    tail[m * group:(m + 1) * group] = laid(total)

    def wait_solved(t):
        pltpu.make_async_copy(x_in.at[t], x_in.at[t], r_sem.at[t]).wait()

    @pl.when(row < blk)
    def _():
        wait_solved(0)
        send_late()

    @pl.loop(0, TICKS)
    def _(t):
        @pl.when(is_lower & (t == 1))
        def _():
            send_late()

        @pl.when(is_next & (t == TICKS - 1) & (row >= SINGLE) & jnp.logical_not(rest_by_diag))
        def _():
            give_rest()

        @pl.when(is_lower & (blk >= t))
        def _():
            tick(t)

    has_tail = is_lower & (blk >= TICKS - 1)

    @pl.when(has_tail)
    def _():
        @pl.loop(0, owners)
        def _(o):
            give(o, tail.at[o], tail_in.at[slot], ts_sem, t_sem.at[slot])

    @pl.loop(0, SINGLE)
    def _(t):
        @pl.when((row >= t) & ((t > 0) | (row >= blk)))
        def _():
            wait_solved(t)

    @pl.when(row >= SINGLE)
    def _():
        pltpu.make_async_copy(x_in.at[rest], x_in.at[rest], r_sem.at[SINGLE]).wait()

    @pl.loop(0, blocks)
    def _(s):
        t = row - s

        @pl.when((t >= 0) & (t < TICKS))
        def _():
            grad_own[s] = x_in[jnp.clip(t, 0, TICKS - 1)].astype(F32)[:rows]

        @pl.when(t >= TICKS)
        def _():
            ref = tail_in.at[jnp.minimum(s, tail_in.shape[0] - 1)]
            pltpu.make_async_copy(ref, ref, t_sem.at[jnp.minimum(s, tail_in.shape[0] - 1)]).wait()
            grad_own[s] = grad_own[s] - ref[...].astype(F32)[:rows]

    for p in range(blocks):
        out_ref[:, p * width:(p + 1) * width] = grad_own[starts_ref[p]]

    for t in range(2, TICKS):
        sent_grad(t)

    for h in range(2):
        @pl.when(is_diag & moved & (half == h))
        def _():
            for k in range(per):
                diag_copy(h, k).wait_send()

    @pl.when(is_lower)
    def _():
        tile_copy.wait_send()

    @pl.loop(0, TICKS)
    def _(t):
        for m in range(CHUNKS):
            @pl.when((row >= t) & ((is_diag & (t < limit)) | (is_next & (t >= limit))))
            def _():
                res_copy(t, m).wait_send()
                for k in range(2):
                    @pl.when(row + 1 + k < blocks)
                    def _():
                        solved_copy(t, m, k).wait_send()

            @pl.when(is_next & (row >= t) & (t > 0) & (t < limit))
            def _():
                first_copy(t, m).wait_send()

            @pl.when(is_lower & (blk >= t))
            def _():
                vec_copy(t, m).wait_send()

                @pl.when(row + 2 < blocks)
                def _():
                    forward_copy(t, m).wait_send()

                @pl.when((t < TICKS - 1) & into_next)
                def _():
                    near_sum(t, m).wait_send()

                @pl.when((t < TICKS - 1) & (row > blk + 2))
                def _():
                    far_sum(t, m).wait_send()

    def sent_all(ref_all, ref_less, sem):
        @pl.when(my_group == half)
        def _():
            pltpu.make_async_copy(ref_less, ref_less, sem).wait()

        @pl.when(my_group != half)
        def _():
            pltpu.make_async_copy(ref_all, ref_all, sem).wait()

    less = pl.ds(0, owners - 1)

    @pl.when(has_tail)
    def _():
        sent_all(tail, tail.at[less], ts_sem)

    @pl.loop(0, SINGLE)
    def _(t):
        @pl.when((row >= t) & ((is_diag & (t < limit)) | (is_next & (t >= limit))))
        def _():
            sent_all(x_ret.at[t], x_ret.at[t, less], rs_sem.at[t])

    @pl.when((row >= SINGLE) & ((is_diag & rest_by_diag) | (is_next & jnp.logical_not(rest_by_diag))))
    def _():
        sent_all(x_ret.at[rest], x_ret.at[rest, less], rs_sem.at[SINGLE])


def body(factor, gradient, starts):
    blocks = starts.shape[0]
    rows = gradient.shape[0]
    width = gradient.shape[1] // blocks
    tile_rows, half_rows = factor.shape
    owners = blocks
    vmem = pltpu.VMEM
    dma = pltpu.SemaphoreType.DMA
    spare = max(blocks - TICKS, 1)
    scratch = [
        vmem((2, half_rows, half_rows), BF16),
        vmem((tile_rows, half_rows), BF16),
        vmem((2, half_rows, half_rows), BF16),
        vmem((TICKS, 2, half_rows, width), BF16),
        vmem((TICKS, 2, half_rows, width), BF16),
        vmem((TICKS, half_rows, width), BF16),
        vmem((TICKS, half_rows, width), F32),
        vmem((TICKS, half_rows, width), F32),
        vmem((TICKS, half_rows, width), BF16),
        vmem((TICKS, half_rows, width), BF16),
        vmem((TICKS, half_rows, width), BF16),
        vmem((TICKS, half_rows, width), BF16),
        vmem((half_rows, width), F32),
        vmem((owners, 64, width), BF16),
        vmem(gradient.shape, F32),
        vmem((blocks, rows, width), F32),
        vmem((blocks, rows, width), F32),
        vmem((TICKS, 64, width), BF16),
        vmem((TICKS, owners, 64, width), BF16),
        vmem((TICKS, owners, 64, width), BF16),
        vmem((TICKS, 64, width), BF16),
        vmem((spare, 64, width), BF16),
        dma, dma, dma((2,)), dma((half_rows // 128,)), dma((half_rows // 128,)), dma((TICKS,)), dma((TICKS,)),
        dma((2, TICKS, CHUNKS)), dma((2, TICKS, CHUNKS)), dma((2, TICKS, CHUNKS)),
        dma((TICKS, CHUNKS)), dma((TICKS, CHUNKS)), dma((2, TICKS, CHUNKS)), dma((2, TICKS, CHUNKS)),
        dma((TICKS, CHUNKS)), dma((TICKS, CHUNKS)), dma((TICKS,)), dma((TICKS,)), dma, dma((spare,)),
    ]
    return pl.pallas_call(
        functools.partial(kernel, blocks),
        out_shape=jax.ShapeDtypeStruct(gradient.shape, F32),
        in_specs=[
            pl.BlockSpec(memory_space=pltpu.SMEM),
            pl.BlockSpec(memory_space=pl.ANY),
            pl.BlockSpec(memory_space=pl.ANY),
        ],
        out_specs=pl.BlockSpec(memory_space=pltpu.VMEM),
        scratch_shapes=scratch,
        compiler_params=pltpu.CompilerParams(
            collective_id=0, has_side_effects=True, vmem_limit_bytes=62 * 1024 * 1024
        ),
        cost_estimate=pl.CostEstimate(
            flops=2 * TICKS * tile_rows * half_rows * width,
            bytes_accessed=2 * tile_rows * half_rows, transcendentals=0,
        ),
    )(starts, gradient, factor)


def solution(mesh):
    in_specs = (P("row", "col"), P(("row", "col"), None), P())
    out_specs = P(("row", "col"), None)
    return jax.shard_map(body, mesh=mesh, in_specs=in_specs, out_specs=out_specs, check_vma=False)
```
